256 devices in a mesh: dp: 4 (over x), node: 8 (over y, core), local: 8 (over z).
Axes of the slice: x: 4, y: 4, z: 8, core: 2. Of those that a mesh axis runs over, the one named last changes fastest.
Arguments:
- tokens: bfloat16 [4096, 3584], P(('dp', 'node', 'local')), may hold values from -6 to 6
- cotangent: bfloat16 [4096, 3584], P(('dp', 'node', 'local')), may hold values from -6 to 6
- routes: int32 [4096, 8], P(('dp', 'node', 'local')), may hold values from 0 to 63, as said below
- gates: bfloat16 [4096, 8], P(('dp', 'node', 'local')), may hold values from 0.099609375 to 0.5
- w_gate: bfloat16 [64, 3584, 1024], P(('node', 'local'), None, 'dp'), may hold values from -0.09375 to 0.09375
- w_up: bfloat16 [64, 3584, 1024], P(('node', 'local'), None, 'dp'), may hold values from -0.09375 to 0.09375
- w_down: bfloat16 [64, 1024, 3584], P(('node', 'local'), 'dp'), may hold values from -0.1875 to 0.1875
Outputs:
- d_tokens: bfloat16 [4096, 3584], P(('dp', 'node', 'local'))
- d_gates: float32 [4096, 8], P(('dp', 'node', 'local'))
- grad_gate: bfloat16 [64, 3584, 1024], P(('node', 'local'), None, 'dp')
- grad_up: bfloat16 [64, 3584, 1024], P(('node', 'local'), None, 'dp')
- grad_down: bfloat16 [64, 1024, 3584], P(('node', 'local'), 'dp')
The draws below stay inside these ranges and needn't reach their ends.
Inputs may be any that keep to these rules, and one draw needn't show every extreme that they name: `routes`: each row names 8 different experts, 2 in each of exactly 4 node groups, expert e lying in node group e // 8. Among the rows of one device each node group is named by exactly 8 rows and no expert by more than 3 rows; in every draw each node group has an expert named by exactly 3 rows of every device.
All inputs are finite; a program needn't handle non-finite values.
Results may differ from the reference program's by a relative error of at most 0.0075.
Values may be sent and summed in bfloat16 or wider, within the bound.
No kernel may reach another device: no remote copies, remote signals or barrier semaphores. Data moves between devices by JAX's collectives and lax.ppermute only.
A program may use at most 128 MiB of HBM per device.

```python
import jax
import jax.numpy as jnp
from jax import lax

D = 3584
FF = 1024
TOP = 8
TOK_DEV = 16
EXPERTS = 64
NODE_GROUPS = 8
EXPERTS_IN_GROUP = 8
BLOCKS = 256
TOKENS = 4096
GROUPS = 4
PER_GROUP = 2
GROUP_ROWS = 8
MOST = 3


def draw_routes(key, part):
    key = jax.random.fold_in(key, 7)
    key_pop, key_hot, key_noise, key_perm = jax.random.split(key, 4)
    expert_preference = jax.random.randint(key_pop, (NODE_GROUPS, EXPERTS_IN_GROUP), 0, 4)
    favored_column = jax.random.randint(key_hot, (NODE_GROUPS,), 0, EXPERTS_IN_GROUP)
    expert_columns = jnp.arange(EXPERTS_IN_GROUP)
    favored_increment = jnp.where(expert_columns[None, :] == favored_column[:, None], 16, 0)
    block_jitter = jax.random.randint(key_noise, (BLOCKS, NODE_GROUPS, EXPERTS_IN_GROUP), 0, 8)
    ranking_score = ((expert_preference + favored_increment)[None] * 8 + block_jitter) * EXPERTS_IN_GROUP + expert_columns
    ranked = jnp.argsort(-ranking_score, axis=2)
    perm_keys = jax.random.split(key_perm, BLOCKS)
    group_perm = jax.vmap(lambda block_key: jax.random.permutation(block_key, NODE_GROUPS))(perm_keys)
    rank_ids = jnp.arange(EXPERTS_IN_GROUP)
    rank_loads = jnp.minimum(MOST, jnp.maximum(0, GROUP_ROWS * PER_GROUP - rank_ids * MOST))
    load_ends = jnp.cumsum(rank_loads)
    token_ids = jnp.arange(TOK_DEV)
    group_slots = jnp.arange(NODE_GROUPS)
    member = ((group_slots[None, :] - token_ids[:, None]) % NODE_GROUPS < GROUPS).astype(jnp.int32)
    before = jnp.cumsum(member, axis=0) - member
    block_ids = jnp.arange(BLOCKS)
    chosen = []
    for turn_index in range(GROUPS):
        slot_of = (token_ids + turn_index) % NODE_GROUPS
        member_rank = before[token_ids, slot_of]
        group_ids = group_perm[:, slot_of]
        for pick_index in range(PER_GROUP):
            position = member_rank + pick_index * GROUP_ROWS
            rank_index = jnp.sum((load_ends[None, :] <= position[:, None]).astype(jnp.int32), axis=1)
            local_pick = ranked[block_ids[:, None], group_ids, rank_index[None, :]]
            chosen.append(group_ids * EXPERTS_IN_GROUP + local_pick)
    return jnp.stack(chosen, axis=2).reshape(TOKENS, TOP).astype(jnp.int32)


def levels(stream_key, dims, cuts, low, top_value):
    loudness, own = 1.0, jax.random.fold_in(stream_key, 6)
    for axis_at, shards_of in cuts:
        heights = jnp.exp(jax.random.uniform(jax.random.fold_in(own, axis_at), (shards_of,), jnp.float32, low / len(cuts), top_value / len(cuts)))
        loudness = loudness * jnp.repeat(heights, dims[axis_at] // shards_of).reshape([-1 if axis == axis_at else 1 for axis in range(len(dims))])
    return loudness


def scatter_about(stream_key, extent, scale, limit, shards=(), kind=jnp.bfloat16):
    drawn = jax.random.normal(stream_key, extent, jnp.float32) * scale
    if len(shards) > 0:
        drawn = levels(stream_key, extent, shards, -0.22, 0.18) * drawn
    return jnp.clip(drawn, min=-limit, max=limit).astype(kind)


def setup_inputs(seed: int = 0) -> dict:
    keys = jax.random.split(jax.random.key(seed), 8)
    return {
        "tokens": scatter_about(keys[0], (TOKENS, D), 1.0, 6.0, ((0, 256),)),
        "cotangent": scatter_about(keys[1], (TOKENS, D), 1.0, 6.0, ((0, 256),)),
        "routes": draw_routes(jax.random.fold_in(keys[7], 71), 0),
        "gates": jnp.clip(0.099609375 + 0.40039062 * jax.random.uniform(keys[3], (TOKENS, TOP), jnp.float32) ** levels(keys[3], (TOKENS, TOP), ((0, 256),), -0.2, 0.2), 0.099609375, 0.5).astype(jnp.bfloat16),
        "w_gate": scatter_about(keys[4], (EXPERTS, D, FF), D ** -0.5, 0.09375, ((0, 64), (2, 4))),
        "w_up": scatter_about(keys[5], (EXPERTS, D, FF), D ** -0.5, 0.09375, ((0, 64), (2, 4))),
        "w_down": scatter_about(keys[6], (EXPERTS, FF, D), FF ** -0.5, 0.1875, ((0, 64), (1, 4))),
    }


def expert_math(rows_x, rows_dy, gate_mat, up_mat, down_mat):
    gate_pre = jnp.dot(rows_x, gate_mat, preferred_element_type=jnp.float32)
    up_pre = jnp.dot(rows_x, up_mat, preferred_element_type=jnp.float32)
    sigmoid_gate = jax.nn.sigmoid(gate_pre)
    activated = gate_pre * sigmoid_gate
    hidden = (activated * up_pre).astype(jnp.bfloat16)
    expert_out = jnp.dot(hidden, down_mat, preferred_element_type=jnp.float32)
    gate_rows = jnp.sum(expert_out * rows_dy.astype(jnp.float32), axis=1)
    d_hidden = lax.dot_general(rows_dy, down_mat, (((1,), (1,)), ((), ())), preferred_element_type=jnp.float32)
    d_gate_pre = (d_hidden * up_pre * sigmoid_gate * (1.0 + gate_pre * (1.0 - sigmoid_gate))).astype(jnp.bfloat16)
    d_up_pre = (d_hidden * activated).astype(jnp.bfloat16)
    d_input = lax.dot_general(d_gate_pre, gate_mat, (((1,), (1,)), ((), ())), preferred_element_type=jnp.float32)
    d_input = d_input + lax.dot_general(d_up_pre, up_mat, (((1,), (1,)), ((), ())), preferred_element_type=jnp.float32)
    grad_g = lax.dot_general(rows_x, d_gate_pre, (((0,), (0,)), ((), ())), preferred_element_type=jnp.float32)
    grad_u = lax.dot_general(rows_x, d_up_pre, (((0,), (0,)), ((), ())), preferred_element_type=jnp.float32)
    grad_d = lax.dot_general(hidden, rows_dy, (((0,), (0,)), ((), ())), preferred_element_type=jnp.float32)
    return d_input, gate_rows, grad_g, grad_u, grad_d


def reference(tokens, cotangent, routes, gates, w_gate, w_up, w_down):
    flat_routes = routes.reshape(-1)
    flat_gates = gates.reshape(-1).astype(jnp.float32)
    capacity = BLOCKS * MOST
    slot_lanes = jnp.arange(capacity, dtype=jnp.int32)

    def per_expert(totals, expert):
        grad_acc, gate_acc = totals
        matches = flat_routes == expert
        live_count = jnp.sum(matches.astype(jnp.int32))
        pick_index = jnp.nonzero(matches, size=capacity, fill_value=0)[0].astype(jnp.int32)
        valid = slot_lanes < live_count
        token_index = (pick_index // TOP).astype(jnp.int32)
        rows_x = jnp.where(valid[:, None], tokens[token_index], jnp.zeros_like(tokens[:1]))
        rows_dy = jnp.where(valid[:, None], cotangent[token_index], jnp.zeros_like(cotangent[:1]))
        d_input, gate_rows, grad_g, grad_u, grad_d = expert_math(rows_x, rows_dy, w_gate[expert], w_up[expert], w_down[expert])
        weight_col = jnp.where(valid, flat_gates[pick_index], jnp.float32(0.0))
        grad_acc = grad_acc.at[token_index].add(weight_col[:, None] * d_input)
        gate_acc = gate_acc.at[pick_index].add(jnp.where(valid, gate_rows, jnp.float32(0.0)))
        return (grad_acc, gate_acc), (grad_g.astype(jnp.bfloat16), grad_u.astype(jnp.bfloat16), grad_d.astype(jnp.bfloat16))

    start = (jnp.zeros((TOKENS, D), jnp.float32), jnp.zeros((TOKENS * TOP,), jnp.float32))
    (grad_acc, gate_acc), (grad_gate, grad_up, grad_down) = lax.scan(per_expert, start, jnp.arange(EXPERTS, dtype=jnp.int32))
    return grad_acc.astype(jnp.bfloat16), gate_acc.reshape(TOKENS, TOP), grad_gate, grad_up, grad_down
```

```python
import jax
import jax.numpy as jnp
from jax import lax
from jax.sharding import PartitionSpec as P

F32 = jnp.float32
BF16 = jnp.bfloat16
GROUP_MAX = 4
CHUNK_PARTS = (1, 2, 2, 2)
BACK_PARTS = (2, 2, 3)
EXTRA = 128


def splits(width, parts):
    unit = width // sum(parts)
    edges = [0]
    for part in parts:
        edges.append(edges[-1] + unit * part)
    return list(zip(edges[:-1], edges[1:]))


def shift(value, step):
    size = lax.axis_size("dp")
    return lax.ppermute(value, "dp", [(i, (i + step) % size) for i in range(size)])


def swap(value, axis):
    return lax.all_to_all(value, axis, split_axis=0, concat_axis=0, tiled=True)


def dot(a, b, ca, cb):
    return lax.dot_general(a, b, (((ca,), (cb,)), ((), ())), preferred_element_type=F32)


def high_low(value):
    high = lax.reduce_precision(value, 8, 7)
    return high, value - high


def extra_block(columns):
    rows = columns[0].shape[0]
    lane = lax.broadcasted_iota(jnp.int32, (rows, EXTRA), 1)
    out = jnp.zeros((rows, EXTRA), F32)
    for index, column in enumerate(columns):
        out = jnp.where(lane == index, column[:, None].astype(F32), out)
    return out


def local(tokens, cotangent, routes, gates, w_gate, w_up, w_down):
    tok_dev, width = tokens.shape
    top = routes.shape[1]
    nodes = lax.axis_size("node")
    locals_ = lax.axis_size("local")
    group_rows = tok_dev * min(GROUP_MAX, nodes) // nodes
    most = max(2, tok_dev * top // (nodes * locals_) + 1)
    mid_rows = nodes * group_rows
    seat = nodes * min(most, group_rows)
    rows = locals_ * seat

    group = routes // locals_
    place = routes % locals_
    in_group = group[:, :, None] == jnp.arange(nodes, dtype=jnp.int32)
    in_group_i = in_group.astype(jnp.int32)
    order = jnp.cumsum(in_group_i, axis=1) - in_group_i
    pick_a = jnp.logical_and(in_group, order == 0)
    pick_b = jnp.logical_and(in_group, order == 1)
    member = jnp.any(in_group, axis=1)
    member_i = member.astype(jnp.int32)
    rank = jnp.cumsum(member_i, axis=0) - member_i
    seat_hot = jnp.logical_and(
        member.T[:, None, :],
        rank.T[:, None, :] == jnp.arange(group_rows, dtype=jnp.int32)[None, :, None],
    )
    first_hot = seat_hot.reshape(mid_rows, tok_dev).astype(BF16)

    def of_pick(pick, value):
        return jnp.sum(jnp.where(pick, value.astype(F32)[:, :, None], 0.0), axis=1)

    facts = [
        of_pick(pick_a, place), of_pick(pick_b, place),
        of_pick(pick_a, gates), of_pick(pick_b, gates),
    ]
    facts = [
        jnp.sum(jnp.where(seat_hot, fact.T[:, None, :], 0.0), axis=2).reshape(mid_rows)
        for fact in facts
    ]
    meta = extra_block(facts).astype(BF16)

    chunks = splits(width, CHUNK_PARTS)
    sent = []
    for low, high in chunks:
        both = jnp.concatenate([tokens[:, low:high], cotangent[:, low:high]], axis=1)
        sent.append(dot(first_hot, both, 1, 0).astype(BF16))
    head = jnp.concatenate([meta, sent[0]], axis=1)
    tail = jnp.concatenate(sent[1:], axis=1)
    head = swap(head.reshape(nodes, group_rows, -1), "node").reshape(mid_rows, -1)
    tail = swap(tail.reshape(nodes, group_rows, -1), "node").reshape(mid_rows, -1)
    meta, mid = head[:, :EXTRA], [head[:, EXTRA:]]
    base = chunks[1][0]
    for low, high in chunks[1:]:
        mid.append(tail[:, 2 * (low - base):2 * (high - base)])

    place_a, place_b = meta[:, 0], meta[:, 1]
    gate_a, gate_b = meta[:, 2], meta[:, 3]
    slots = jnp.arange(locals_, dtype=jnp.int32).astype(BF16)
    hit_a = place_a[:, None] == slots
    hit_b = place_b[:, None] == slots
    hit = jnp.logical_or(hit_a, hit_b)
    hit_i = hit.astype(jnp.int32)
    rank_two = jnp.cumsum(hit_i, axis=0) - hit_i
    seats = rank_two[:, :, None] == jnp.arange(seat, dtype=jnp.int32)
    table_a = jnp.logical_and(hit_a[:, :, None], seats).reshape(mid_rows, rows)
    table_b = jnp.logical_and(hit_b[:, :, None], seats).reshape(mid_rows, rows)
    second_hot = jnp.logical_or(table_a, table_b).astype(BF16)
    combine = (
        jnp.where(table_a, gate_a[:, None], 0.0) + jnp.where(table_b, gate_b[:, None], 0.0)
    ).astype(BF16)

    gate_up_mat = jnp.concatenate([w_gate[0], w_up[0]], axis=1)
    down_mat = w_down[0]
    hidden_width = down_mat.shape[0]

    gate_up = None
    d_hidden = None
    rows_x, rows_dy = [], []
    for index, (low, high) in enumerate(chunks):
        size = high - low
        out = dot(second_hot, mid[index], 0, 0).astype(BF16)
        own = swap(out.reshape(locals_, seat, 2 * size), "local").reshape(rows, 2 * size)
        from_up = shift(own, -1)
        from_down = shift(own, 1)
        far_one = shift(from_up[:, :size], -1)
        far_two = shift(from_down[:, size:], 1)
        part_x = jnp.concatenate(
            [own[:, :size], from_up[:, :size], from_down[:, :size], far_one], axis=0
        )
        part_dy = jnp.concatenate(
            [own[:, size:], from_up[:, size:], from_down[:, size:], far_two], axis=0
        )
        more = dot(part_x, gate_up_mat[low:high], 1, 0)
        gate_up = more if gate_up is None else gate_up + more
        more = dot(part_dy, down_mat[:, low:high], 1, 1)
        d_hidden = more if d_hidden is None else d_hidden + more
        rows_x.append(part_x)
        rows_dy.append(part_dy)

    gate_pre = gate_up[:, :hidden_width]
    up_pre = gate_up[:, hidden_width:]
    sigmoid_gate = jax.nn.sigmoid(gate_pre)
    activated = gate_pre * sigmoid_gate
    hidden = (activated * up_pre).astype(BF16)
    gate_rows = jnp.sum(hidden.astype(F32) * d_hidden, axis=1)
    d_gate_pre = (
        d_hidden * up_pre * sigmoid_gate * (1.0 + gate_pre * (1.0 - sigmoid_gate))
    ).astype(BF16)
    d_up_pre = (d_hidden * activated).astype(BF16)
    d_pre = jnp.concatenate([d_gate_pre, d_up_pre], axis=1)

    pieces = [d_pre[i * rows:(i + 1) * rows] for i in range(4)]
    gate_pieces = [gate_rows[i * rows:(i + 1) * rows] for i in range(4)]
    back_chunks = splits(width, BACK_PARTS)
    returned = []
    for index, (low, high) in enumerate(back_chunks):
        last = index == len(back_chunks) - 1
        mat = gate_up_mat[low:high]

        def part(which):
            value = dot(pieces[which], mat, 1, 1)
            if last:
                value = jnp.concatenate(
                    [value, extra_block(high_low(gate_pieces[which]))], axis=1
                )
            return value

        size = high - low + (EXTRA if last else 0)
        half = (size // 2) // 128 * 128
        far = part(3).astype(BF16)
        relay_one = shift(far[:, :half], 1)
        relay_two = shift(far[:, half:], -1)
        to_up = part(1) + jnp.pad(relay_one.astype(F32), ((0, 0), (0, size - half)))
        to_down = part(2) + jnp.pad(relay_two.astype(F32), ((0, 0), (half, 0)))
        came_one = shift(to_up.astype(BF16), 1)
        came_two = shift(to_down.astype(BF16), -1)
        total = part(0) + came_one.astype(F32) + came_two.astype(F32)
        back = swap(total.astype(BF16).reshape(locals_, seat, size), "local").reshape(rows, size)
        if last:
            body, extra = back[:, :-EXTRA], back[:, -EXTRA:]
            got_a = dot(table_a.astype(BF16), extra, 1, 0)
            got_b = dot(table_b.astype(BF16), extra, 1, 0)
            grads = high_low(got_a[:, 0] + got_a[:, 1]) + high_low(got_b[:, 0] + got_b[:, 1])
            value = jnp.concatenate([dot(combine, body, 1, 0), extra_block(grads)], axis=1)
        else:
            value = dot(combine, back, 1, 0)
        returned.append(value.astype(BF16))

    early = jnp.concatenate(returned[:-1], axis=1)
    late = returned[-1]
    early = swap(early.reshape(nodes, group_rows, -1), "node").reshape(mid_rows, -1)
    late = swap(late.reshape(nodes, group_rows, -1), "node").reshape(mid_rows, -1)
    d_tokens = jnp.concatenate(
        [dot(first_hot, early, 0, 0), dot(first_hot, late[:, :-EXTRA], 0, 0)], axis=1
    ).astype(BF16)
    extra = late[:, -EXTRA:].astype(F32)
    grad_a = (extra[:, 0] + extra[:, 1]).reshape(nodes, group_rows)
    grad_b = (extra[:, 2] + extra[:, 3]).reshape(nodes, group_rows)
    tok_a = jnp.sum(jnp.where(seat_hot, grad_a[:, :, None], 0.0), axis=1).T
    tok_b = jnp.sum(jnp.where(seat_hot, grad_b[:, :, None], 0.0), axis=1).T
    d_gates = jnp.sum(
        jnp.where(pick_a, tok_a[:, None, :], 0.0) + jnp.where(pick_b, tok_b[:, None, :], 0.0),
        axis=2,
    )

    grad_gate = jnp.concatenate(
        [dot(part_x, d_gate_pre, 0, 0).astype(BF16) for part_x in rows_x], axis=0
    )
    grad_up = jnp.concatenate(
        [dot(part_x, d_up_pre, 0, 0).astype(BF16) for part_x in rows_x], axis=0
    )
    grad_down = jnp.concatenate(
        [dot(hidden, part_dy, 0, 0).astype(BF16) for part_dy in rows_dy], axis=1
    )
    return d_tokens, d_gates, grad_gate[None], grad_up[None], grad_down[None]


def solution(mesh):
    rows = P(("dp", "node", "local"), None)
    wide = P(("node", "local"), None, "dp")
    tall = P(("node", "local"), "dp", None)
    return jax.shard_map(
        local,
        mesh=mesh,
        in_specs=(rows, rows, rows, rows, wide, wide, tall),
        out_specs=(rows, rows, wide, wide, tall),
        check_vma=False,
    )
```

```python
import jax
import jax.numpy as jnp
from jax import lax
from jax.sharding import PartitionSpec as P

F32 = jnp.float32
BF16 = jnp.bfloat16
GROUP_MAX = 4
LANES = 128


def shift(value, step):
    size = lax.axis_size("dp")
    return lax.ppermute(value, "dp", [(i, (i + step) % size) for i in range(size)])


def swap(value):
    rows, width = value.shape
    value = value.reshape(rows, width // LANES, LANES)
    value = lax.all_to_all(value, ("node", "local"), split_axis=0, concat_axis=0, tiled=True)
    return value.reshape(rows, width)


def dot(a, b, ca, cb):
    return lax.dot_general(a, b, (((ca,), (cb,)), ((), ())), preferred_element_type=F32)


def high_low(value):
    high = lax.reduce_precision(value, 8, 7)
    return high, value - high


def extra_block(columns):
    rows = columns[0].shape[0]
    lane = lax.broadcasted_iota(jnp.int32, (rows, LANES), 1)
    out = jnp.zeros((rows, LANES), F32)
    for index, column in enumerate(columns):
        out = jnp.where(lane == index, column[:, None], out)
    return out


def local(tokens, cotangent, routes, gates, w_gate, w_up, w_down):
    tok_dev, width = tokens.shape
    top = routes.shape[1]
    nodes = lax.axis_size("node")
    experts = nodes * lax.axis_size("local")
    group_rows = tok_dev * min(GROUP_MAX, nodes) // nodes
    most = min(group_rows, max(2, tok_dev * top // experts + 1))

    named = routes[:, :, None] == jnp.arange(experts, dtype=jnp.int32)
    member = jnp.any(named, axis=1)
    member_i = member.astype(jnp.int32)
    rank = jnp.cumsum(member_i, axis=0) - member_i
    weight = jnp.sum(jnp.where(named, gates.astype(F32)[:, :, None], 0.0), axis=1)
    seats = [jnp.logical_and(member, rank == turn) for turn in range(most)]

    both = jnp.concatenate([tokens, cotangent], axis=1)
    down_mat = w_down[0]
    hidden_width = down_mat.shape[0]
    tied = jnp.concatenate([w_gate[0], w_up[0], jnp.zeros((width, LANES), BF16)], axis=1)
    eye = jnp.eye(LANES, 2 * hidden_width + LANES, 2 * hidden_width, dtype=BF16)
    back_mat = jnp.concatenate([tied, eye], axis=0)
    half = experts // 2

    def pick(turn, source):
        return dot(seats[turn].astype(BF16), source, 0, 0).astype(BF16)

    def ring_one(own):
        return shift(own, -1), shift(own, 1)

    def ring_two(up, down):
        return shift(up[:half], -1), shift(down[half:], 1)

    def forward(own, up, down, far_one, far_two):
        blocks = (far_one, far_two, up, down, own)
        part_x = jnp.concatenate([block[:, :width] for block in blocks], axis=0)
        part_dy = jnp.concatenate([block[:, width:] for block in blocks], axis=0)
        part_x, part_dy = lax.optimization_barrier((part_x, part_dy))
        gate_pre = dot(part_x, w_gate[0], 1, 0)
        up_pre = dot(part_x, w_up[0], 1, 0)
        d_hidden = dot(part_dy, down_mat, 1, 1)
        sigmoid_gate = jax.nn.sigmoid(gate_pre)
        activated = gate_pre * sigmoid_gate
        hidden = (activated * up_pre).astype(BF16)
        gate_rows = jnp.sum(hidden.astype(F32) * d_hidden, axis=1)
        d_gate_pre = (
            d_hidden * up_pre * sigmoid_gate * (1.0 + gate_pre * (1.0 - sigmoid_gate))
        ).astype(BF16)
        d_up_pre = (d_hidden * activated).astype(BF16)
        extra = extra_block(high_low(gate_rows)).astype(BF16)
        d_pre = jnp.concatenate([d_gate_pre, d_up_pre, extra], axis=1)
        d_input = dot(d_pre, back_mat, 1, 1)
        far, to_up, to_down, mine = [d_input[i * experts:(i + 1) * experts] for i in range(4)]
        return (part_x, part_dy, d_gate_pre, d_up_pre, hidden), (far.astype(BF16), to_up, to_down, mine)

    def back_one(far):
        return shift(far[:half], 1), shift(far[half:], -1)

    def back_two(relays, parts):
        _, to_up, to_down, _ = parts
        to_up = jnp.concatenate([to_up[:half] + relays[0].astype(F32), to_up[half:]], axis=0)
        to_down = jnp.concatenate([to_down[:half], to_down[half:] + relays[1].astype(F32)], axis=0)
        return shift(to_up.astype(BF16), 1), shift(to_down.astype(BF16), -1)

    def back_sum(parts, *came):
        total = parts[3]
        for value in came:
            total = total + value.astype(F32)
        return total.astype(BF16)

    def grads(saved, sums):
        part_x, part_dy, d_gate_pre, d_up_pre, hidden = saved
        return (
            sums[0] + dot(part_x, d_gate_pre, 0, 0),
            sums[1] + dot(part_x, d_up_pre, 0, 0),
            sums[2] + dot(hidden, part_dy, 0, 0),
        )

    bar = lax.optimization_barrier

    own0 = swap(pick(0, both))
    both1, own0 = bar((both, own0))
    x0 = ring_one(own0)
    own1 = swap(pick(1, both1))
    y0 = ring_two(*x0)
    own0, x0, y0, own1, both2 = bar((own0, x0, y0, own1, both1))
    x1 = ring_one(own1)
    own2 = swap(pick(2, both2))
    saved0, parts0 = forward(own0, *x0, *y0)
    own1, x1, parts0 = bar((own1, x1, parts0))
    y1 = ring_two(*x1)
    r0 = back_one(parts0[0])
    own1, x1, y1, r0, own2 = bar((own1, x1, y1, r0, own2))
    x2 = ring_one(own2)
    s0 = back_two(r0, parts0)
    saved1, parts1 = forward(own1, *x1, *y1)
    x2, parts1, own2, s0 = bar((x2, parts1, own2, s0))
    y2 = ring_two(*x2)
    r1 = back_one(parts1[0])
    total0 = back_sum(parts0, *s0)
    home0 = swap(total0)
    x2, y2, r1 = bar((x2, y2, r1))
    s1 = back_two(r1, parts1)
    saved2, parts2 = forward(own2, *x2, *y2)
    t2 = shift(parts2[0], 2)
    s2 = shift(parts2[1].astype(BF16), 1), shift(parts2[2].astype(BF16), -1)
    s1, home0, parts2 = bar((s1, home0, parts2))
    total1 = back_sum(parts1, *s1)
    home1 = swap(total1)
    saved0, saved1, saved2, _ = bar((saved0, saved1, saved2, total1))
    sums = grads(saved1, grads(saved0, (0.0, 0.0, 0.0)))
    total2 = back_sum(parts2, t2, *s2)
    total2, home1, sums = bar((total2, home1, sums))
    home2 = swap(total2)
    saved2, _ = bar((saved2, total2))
    grad_gate, grad_up, grad_down = grads(saved2, sums)
    returned = [home0, home1, home2]

    d_tokens = 0.0
    d_weight = 0.0
    for seat, back in zip(seats, returned):
        scaled = jnp.where(seat, weight, 0.0).astype(BF16)
        d_tokens = d_tokens + dot(scaled, back[:, :width], 1, 0)
        extra = back[:, width:].astype(F32)
        d_weight = d_weight + jnp.where(seat, (extra[:, 0] + extra[:, 1])[None, :], 0.0)
    d_gates = jnp.sum(jnp.where(named, d_weight[:, None, :], 0.0), axis=2)
    grad_gate, grad_up, grad_down = [
        value.astype(BF16)[None] for value in (grad_gate, grad_up, grad_down)
    ]
    return d_tokens.astype(BF16), d_gates, grad_gate, grad_up, grad_down


def solution(mesh):
    rows = P(("dp", "node", "local"), None)
    wide = P(("node", "local"), None, "dp")
    tall = P(("node", "local"), "dp", None)
    return jax.shard_map(
        local,
        mesh=mesh,
        in_specs=(rows, rows, rows, rows, wide, wide, tall),
        out_specs=(rows, rows, wide, wide, tall),
        check_vma=False,
    )
```

```python
import jax
import jax.numpy as jnp
from jax import lax
from jax.experimental import pallas as pl
from jax.experimental.pallas import tpu as pltpu
from jax.sharding import PartitionSpec as P

F32 = jnp.float32
BF16 = jnp.bfloat16
GROUP_MAX = 4
LANES = 128
CHUNK = 1792


def shift(value, step):
    size = lax.axis_size("dp")
    return lax.ppermute(value, "dp", [(i, (i + step) % size) for i in range(size)])


def swap(value):
    return lax.all_to_all(value, ("node", "local"), split_axis=0, concat_axis=0, tiled=True)


def by_device(value, peers):
    return value.reshape(peers, -1, LANES)


def dot(a, b, ca, cb):
    return lax.dot_general(a, b, (((ca,), (cb,)), ((), ())), preferred_element_type=F32)


def expert_kernel(steps, count, *refs):
    x_refs, dy_refs, refs = refs[:count], refs[count:2 * count], refs[2 * count:]
    gate_ref, up_ref, down_ref, d_gate_ref, d_up_ref, hidden_ref = refs[:6]
    out_refs, (gate_acc, up_acc, d_hidden_acc) = refs[6:-3], refs[-3:]

    def put(value, begin):
        first = 0
        for ref in out_refs:
            last = first + ref.shape[0]
            ref[:, pl.ds(begin, value.shape[1])] = value[first:last]
            first = last
    phase, step = pl.program_id(0), pl.program_id(1)

    @pl.when(phase == 0)
    def _():
        @pl.when(step == 0)
        def _():
            gate_acc[...] = jnp.zeros_like(gate_acc)
            up_acc[...] = jnp.zeros_like(up_acc)
            d_hidden_acc[...] = jnp.zeros_like(d_hidden_acc)

        rows_x = jnp.concatenate([ref[...] for ref in x_refs], axis=0)
        rows_dy = jnp.concatenate([ref[...] for ref in dy_refs], axis=0)
        gate_acc[...] += dot(rows_x, gate_ref[...], 1, 0)
        up_acc[...] += dot(rows_x, up_ref[...], 1, 0)
        d_hidden_acc[...] += dot(rows_dy, down_ref[...], 1, 1)

        @pl.when(step == steps - 1)
        def _():
            gate_pre, up_pre, d_hidden = gate_acc[...], up_acc[...], d_hidden_acc[...]
            sigmoid_gate = jax.nn.sigmoid(gate_pre)
            activated = gate_pre * sigmoid_gate
            hidden = (activated * up_pre).astype(BF16)
            hidden_ref[...] = hidden
            d_gate_ref[...] = (
                d_hidden * up_pre * sigmoid_gate * (1.0 + gate_pre * (1.0 - sigmoid_gate))
            ).astype(BF16)
            d_up_ref[...] = (d_hidden * activated).astype(BF16)
            gate_rows = jnp.sum(hidden.astype(F32) * d_hidden, axis=1, keepdims=True)
            high = gate_rows.astype(BF16).astype(F32)
            lane = lax.broadcasted_iota(jnp.int32, (gate_rows.shape[0], LANES), 1)
            extra = jnp.where(lane == 0, high, jnp.where(lane == 1, gate_rows - high, 0.0))
            put(extra.astype(BF16), steps * CHUNK)

    @pl.when(phase == 1)
    def _():
        value = dot(d_gate_ref[...], gate_ref[...], 1, 1) + dot(d_up_ref[...], up_ref[...], 1, 1)
        put(value.astype(BF16), pl.multiple_of(step * CHUNK, CHUNK))


def expert_rows(blocks, sizes, gate_mat, up_mat, down_mat):
    width, hidden_width = gate_mat.shape
    steps = width // CHUNK
    rows = sum(block.shape[0] for block in blocks)
    small = jax.ShapeDtypeStruct((rows, hidden_width), BF16)
    whole = pl.BlockSpec((rows, hidden_width), lambda p, k: (0, 0))

    def part(block, first):
        return pl.BlockSpec(
            (block.shape[0], CHUNK), lambda p, k: (0, first + k * (1 - p) + (steps - 1) * p)
        )

    return pl.pallas_call(
        lambda *refs: expert_kernel(steps, len(blocks), *refs),
        grid=(2, steps),
        in_specs=[part(block, 0) for block in blocks]
        + [part(block, steps) for block in blocks]
        + [
            pl.BlockSpec((CHUNK, hidden_width), lambda p, k: (k, 0)),
            pl.BlockSpec((CHUNK, hidden_width), lambda p, k: (k, 0)),
            pl.BlockSpec((hidden_width, CHUNK), lambda p, k: (0, k * (1 - p) + (steps - 1) * p)),
        ],
        out_specs=[whole] * 3
        + [pl.BlockSpec((size, width + LANES), lambda p, k: (0, 0)) for size in sizes],
        out_shape=[small] * 3
        + [jax.ShapeDtypeStruct((size, width + LANES), BF16) for size in sizes],
        scratch_shapes=[pltpu.VMEM((rows, hidden_width), F32)] * 3,
        compiler_params=pltpu.CompilerParams(vmem_limit_bytes=60 * 1024 * 1024),
        cost_estimate=pl.CostEstimate(flops=1000000, bytes_accessed=1000000, transcendentals=0),
    )(*blocks, *blocks, gate_mat, up_mat, down_mat)


def local(tokens, cotangent, routes, gates, w_gate, w_up, w_down):
    tok_dev, width = tokens.shape
    top = routes.shape[1]
    nodes = lax.axis_size("node")
    experts = nodes * lax.axis_size("local")
    group_rows = tok_dev * min(GROUP_MAX, nodes) // nodes
    most = min(group_rows, max(2, tok_dev * top // experts + 1))

    named = routes[:, :, None] == jnp.arange(experts, dtype=jnp.int32)
    member = jnp.any(named, axis=1)
    member_i = member.astype(jnp.int32)
    rank = jnp.cumsum(member_i, axis=0) - member_i
    rank = jnp.where(member, rank, most).astype(BF16)
    weight = jnp.sum(jnp.where(named, gates.astype(F32)[:, :, None], 0.0), axis=1)

    def seat_table(first, count):
        columns = experts * count
        spread = lax.broadcasted_iota(jnp.int32, (experts, columns), 1) // count
        spread = (spread == lax.broadcasted_iota(jnp.int32, (experts, columns), 0)).astype(BF16)
        seat_of = lax.broadcasted_iota(jnp.int32, (tok_dev, columns), 1) % count + first
        seats = dot(rank, spread, 1, 0).astype(jnp.int32) == seat_of
        return seats, jnp.where(seats, dot(weight.astype(BF16), spread, 1, 0), 0.0).astype(BF16)

    tables = [seat_table(0, 1), seat_table(1, most - 1)]
    both = jnp.concatenate([tokens, cotangent], axis=1)

    down_mat = w_down[0]
    hidden_width = down_mat.shape[0]
    bar = lax.optimization_barrier

    def pick(turn):
        return by_device(dot(tables[turn][0].astype(BF16), both, 0, 0).astype(BF16), experts)

    def flat(raw, columns):
        return raw.reshape(-1, columns)

    def ring_one(own):
        return shift(own, -1), shift(own, 1)

    def ring_two(up, down):
        size = up.shape[0] // 2
        return shift(up[:size], -1), shift(down[size:], 1)

    def forward(blocks, sizes):
        d_gate_pre, d_up_pre, hidden, *parts = expert_rows(blocks, sizes, w_gate[0], w_up[0], down_mat)
        return (blocks, d_gate_pre, d_up_pre, hidden), parts

    def merge(first, second):
        return (first.astype(F32) + second.astype(F32)).astype(BF16)

    def grads(saved, sums):
        blocks, d_gate_pre, d_up_pre, hidden = saved
        rows_x = jnp.concatenate([block[:, :width] for block in blocks], axis=0)
        rows_dy = jnp.concatenate([block[:, width:] for block in blocks], axis=0)
        return (
            sums[0] + dot(rows_x, d_gate_pre, 0, 0),
            sums[1] + dot(rows_x, d_up_pre, 0, 0),
            sums[2] + dot(hidden, rows_dy, 0, 0),
        )

    raw0 = swap(pick(0))
    send1, raw0 = bar((pick(1), raw0))
    own0 = flat(raw0, 2 * width)
    one0 = ring_one(own0)
    raw1 = swap(send1)
    two0 = ring_two(*one0)
    own0, one0, two0, raw1 = bar((own0, one0, two0, raw1))
    own1 = flat(raw1, 2 * width)
    one1 = ring_one(own1)
    size = own0.shape[0] // 2
    group0, parts0 = forward(two0 + one0 + (own0,), [size] * 6 + [2 * size])
    far_top, far_low, up_top, up_low, down_top, down_low, mine0 = parts0
    relays0 = shift(far_top, 1), shift(far_low, -1)
    own1, one1, relays0, up_top, up_low, down_top, down_low, mine0 = bar(
        (own1, one1, relays0, up_top, up_low, down_top, down_low, mine0)
    )
    up0 = jnp.concatenate([merge(up_top, relays0[0]), up_low], axis=0)
    down0 = jnp.concatenate([down_top, merge(down_low, relays0[1])], axis=0)
    up0, down0, own1, one1 = bar((up0, down0, own1, one1))
    two1 = ring_two(*one1)
    came0 = shift(up0, 1), shift(down0, -1)
    size = own1.shape[0] // 2
    near1, parts1 = forward(one1 + (own1,), [size] * 4 + [2 * size])
    two1, came0, parts1 = bar((two1, came0, parts1))
    up_top, up_low, down_top, down_low, mine = parts1
    early = shift(up_low, 1), shift(down_top, -1)
    far1, far = forward(two1, [size] * 2)
    relays = shift(far[0], 1), shift(far[1], -1)
    came0, _ = bar((came0, far))
    total0 = merge(mine0.astype(F32) + came0[0].astype(F32), came0[1])
    send_home0 = by_device(total0, experts)
    home0 = swap(send_home0)
    came_top = shift(merge(up_top, relays[0]), 1)
    came_low = shift(merge(down_low, relays[1]), -1)
    came_up = jnp.concatenate([came_top, early[0]], axis=0).astype(F32)
    came_down = jnp.concatenate([early[1], came_low], axis=0)
    group0, _ = bar((group0, send_home0))
    sums = grads(group0, (0.0, 0.0, 0.0))
    total1, home0, sums = bar((merge(mine.astype(F32) + came_up, came_down), home0, sums))
    send_home1 = by_device(total1, experts)
    home1 = swap(send_home1)

    d_tokens, d_weight = 0.0, 0.0
    for (seats, combine), home in zip(tables, (home0, home1)):
        home = home.reshape(seats.shape[1], width + LANES)
        d_tokens = d_tokens + dot(combine, home[:, :width], 1, 0)
        extra = home[:, width:].astype(F32)
        d_seat = jnp.where(seats, (extra[:, 0] + extra[:, 1])[None, :], 0.0)
        d_weight = d_weight + jnp.sum(d_seat.reshape(tok_dev, experts, -1), axis=2)
    d_tokens = d_tokens.astype(BF16)
    d_gates = jnp.sum(jnp.where(named, d_weight[:, None, :], 0.0), axis=2)

    near1, far1, _ = bar((near1, far1, send_home1))
    grad_gate, grad_up, grad_down = grads(far1, grads(near1, sums))
    grad_gate, grad_up, grad_down = [
        value.astype(BF16)[None] for value in (grad_gate, grad_up, grad_down)
    ]
    return d_tokens, d_gates, grad_gate, grad_up, grad_down


def solution(mesh):
    rows = P(("dp", "node", "local"), None)
    wide = P(("node", "local"), None, "dp")
    tall = P(("node", "local"), "dp", None)
    return jax.shard_map(
        local,
        mesh=mesh,
        in_specs=(rows, rows, rows, rows, wide, wide, tall),
        out_specs=(rows, rows, wide, wide, tall),
        check_vma=False,
    )
```

```python
import jax
import jax.numpy as jnp
from jax import lax
from jax.experimental import pallas as pl
from jax.experimental.pallas import tpu as pltpu
from jax.sharding import PartitionSpec as P

F32 = jnp.float32
BF16 = jnp.bfloat16
GROUP_MAX = 4
LANES = 128
CHUNK = 1792


def shift(value, step):
    size = lax.axis_size("dp")
    return lax.ppermute(value, "dp", [(i, (i + step) % size) for i in range(size)])


def swap(value):
    return lax.all_to_all(value, ("node", "local"), split_axis=0, concat_axis=0, tiled=True)


def by_device(value, peers):
    return value.reshape(peers, -1, LANES)


def dot(a, b, ca, cb):
    return lax.dot_general(a, b, (((ca,), (cb,)), ((), ())), preferred_element_type=F32)


def expert_kernel(steps, count, *refs):
    x_refs, dy_refs, refs = refs[:count], refs[count:2 * count], refs[2 * count:]
    gate_ref, up_ref, down_ref, d_gate_ref, d_up_ref, hidden_ref = refs[:6]
    out_refs, (gate_acc, up_acc, d_hidden_acc) = refs[6:-3], refs[-3:]

    def put(value, begin):
        first = 0
        for ref in out_refs:
            last = first + ref.shape[0]
            ref[:, pl.ds(begin, value.shape[1])] = value[first:last]
            first = last
    phase, step = pl.program_id(0), pl.program_id(1)

    @pl.when(phase == 0)
    def _():
        @pl.when(step == 0)
        def _():
            gate_acc[...] = jnp.zeros_like(gate_acc)
            up_acc[...] = jnp.zeros_like(up_acc)
            d_hidden_acc[...] = jnp.zeros_like(d_hidden_acc)

        rows_x = jnp.concatenate([ref[...] for ref in x_refs], axis=0)
        rows_dy = jnp.concatenate([ref[...] for ref in dy_refs], axis=0)
        gate_acc[...] += dot(rows_x, gate_ref[...], 1, 0)
        up_acc[...] += dot(rows_x, up_ref[...], 1, 0)
        d_hidden_acc[...] += dot(rows_dy, down_ref[...], 1, 1)

        @pl.when(step == steps - 1)
        def _():
            gate_pre, up_pre, d_hidden = gate_acc[...], up_acc[...], d_hidden_acc[...]
            sigmoid_gate = jax.nn.sigmoid(gate_pre)
            activated = gate_pre * sigmoid_gate
            hidden = (activated * up_pre).astype(BF16)
            hidden_ref[...] = hidden
            d_gate_ref[...] = (
                d_hidden * up_pre * sigmoid_gate * (1.0 + gate_pre * (1.0 - sigmoid_gate))
            ).astype(BF16)
            d_up_ref[...] = (d_hidden * activated).astype(BF16)
            gate_rows = jnp.sum(hidden.astype(F32) * d_hidden, axis=1, keepdims=True)
            high = gate_rows.astype(BF16).astype(F32)
            lane = lax.broadcasted_iota(jnp.int32, (gate_rows.shape[0], LANES), 1)
            extra = jnp.where(lane == 0, high, jnp.where(lane == 1, gate_rows - high, 0.0))
            put(extra.astype(BF16), steps * CHUNK)

    @pl.when(phase == 1)
    def _():
        value = dot(d_gate_ref[...], gate_ref[...], 1, 1) + dot(d_up_ref[...], up_ref[...], 1, 1)
        put(value.astype(BF16), pl.multiple_of(step * CHUNK, CHUNK))


def expert_rows(blocks, sizes, gate_mat, up_mat, down_mat):
    width, hidden_width = gate_mat.shape
    steps = width // CHUNK
    rows = sum(block.shape[0] for block in blocks)
    small = jax.ShapeDtypeStruct((rows, hidden_width), BF16)
    whole = pl.BlockSpec((rows, hidden_width), lambda p, k: (0, 0))

    def part(block, first):
        return pl.BlockSpec(
            (block.shape[0], CHUNK), lambda p, k: (0, first + k * (1 - p) + (steps - 1) * p)
        )

    return pl.pallas_call(
        lambda *refs: expert_kernel(steps, len(blocks), *refs),
        grid=(2, steps),
        in_specs=[part(block, 0) for block in blocks]
        + [part(block, steps) for block in blocks]
        + [
            pl.BlockSpec((CHUNK, hidden_width), lambda p, k: (k, 0)),
            pl.BlockSpec((CHUNK, hidden_width), lambda p, k: (k, 0)),
            pl.BlockSpec((hidden_width, CHUNK), lambda p, k: (0, k * (1 - p) + (steps - 1) * p)),
        ],
        out_specs=[whole] * 3
        + [pl.BlockSpec((size, width + LANES), lambda p, k: (0, 0)) for size in sizes],
        out_shape=[small] * 3
        + [jax.ShapeDtypeStruct((size, width + LANES), BF16) for size in sizes],
        scratch_shapes=[pltpu.VMEM((rows, hidden_width), F32)] * 3,
        compiler_params=pltpu.CompilerParams(vmem_limit_bytes=60 * 1024 * 1024),
        cost_estimate=pl.CostEstimate(flops=1000000, bytes_accessed=1000000, transcendentals=0),
    )(*blocks, *blocks, gate_mat, up_mat, down_mat)


def local(tokens, cotangent, routes, gates, w_gate, w_up, w_down):
    tok_dev, width = tokens.shape
    top = routes.shape[1]
    nodes = lax.axis_size("node")
    experts = nodes * lax.axis_size("local")
    group_rows = tok_dev * min(GROUP_MAX, nodes) // nodes
    most = min(group_rows, max(2, tok_dev * top // experts + 1))

    named = routes[:, :, None] == jnp.arange(experts, dtype=jnp.int32)
    member = jnp.any(named, axis=1)
    member_i = member.astype(jnp.int32)
    rank = jnp.cumsum(member_i, axis=0) - member_i
    rank = jnp.where(member, rank, most).astype(BF16)
    weight = jnp.sum(jnp.where(named, gates.astype(F32)[:, :, None], 0.0), axis=1)

    def seat_table(first, count):
        columns = experts * count
        spread = lax.broadcasted_iota(jnp.int32, (experts, columns), 1) // count
        spread = (spread == lax.broadcasted_iota(jnp.int32, (experts, columns), 0)).astype(BF16)
        seat_of = lax.broadcasted_iota(jnp.int32, (tok_dev, columns), 1) % count + first
        seats = dot(rank, spread, 1, 0).astype(jnp.int32) == seat_of
        return seats, jnp.where(seats, dot(weight.astype(BF16), spread, 1, 0), 0.0).astype(BF16)

    tables = [seat_table(0, 1), seat_table(1, most - 1)]
    both = jnp.concatenate([tokens, cotangent], axis=1)

    down_mat = w_down[0]
    hidden_width = down_mat.shape[0]
    bar = lax.optimization_barrier

    def pick(turn):
        return by_device(dot(tables[turn][0].astype(BF16), both, 0, 0).astype(BF16), experts)

    def flat(raw, columns):
        return raw.reshape(-1, columns)

    def ring_one(own):
        return shift(own, -1), shift(own, 1)

    def ring_two(up, down):
        size = up.shape[0] // 2
        return shift(up[:size], -1), shift(down[size:], 1)

    def forward(blocks, sizes):
        d_gate_pre, d_up_pre, hidden, *parts = expert_rows(blocks, sizes, w_gate[0], w_up[0], down_mat)
        return (blocks, d_gate_pre, d_up_pre, hidden), parts

    def merge(first, second):
        return (first.astype(F32) + second.astype(F32)).astype(BF16)

    def grads(saved, sums):
        blocks, d_gate_pre, d_up_pre, hidden = saved
        rows_x = jnp.concatenate([block[:, :width] for block in blocks], axis=0)
        rows_dy = jnp.concatenate([block[:, width:] for block in blocks], axis=0)
        return (
            sums[0] + dot(rows_x, d_gate_pre, 0, 0),
            sums[1] + dot(rows_x, d_up_pre, 0, 0),
            sums[2] + dot(hidden, rows_dy, 0, 0),
        )

    raw0 = swap(pick(0))
    send1, raw0 = bar((pick(1), raw0))
    own0 = flat(raw0, 2 * width)
    one0 = ring_one(own0)
    raw1 = swap(send1)
    two0 = ring_two(*one0)
    own0, one0, two0, raw1 = bar((own0, one0, two0, raw1))
    own1 = flat(raw1, 2 * width)
    one1 = ring_one(own1)
    size = own0.shape[0] // 2
    group0, parts0 = forward(two0 + one0 + (own0,), [size] * 6 + [2 * size])
    far_top, far_low, up_top, up_low, down_top, down_low, mine0 = parts0
    relays0 = shift(far_top, 1), shift(far_low, -1)
    own1, one1, up_top, up_low, down_top, down_low, mine0 = bar(
        (own1, one1, up_top, up_low, down_top, down_low, mine0)
    )
    two1 = ring_two(*one1)
    up0 = jnp.concatenate([merge(up_top, relays0[0]), up_low], axis=0)
    down0 = jnp.concatenate([down_top, merge(down_low, relays0[1])], axis=0)
    up0, down0, own1, one1 = bar((up0, down0, own1, one1))
    came0 = shift(up0, 1), shift(down0, -1)
    size = own1.shape[0] // 2
    near1, parts1 = forward(one1 + (own1,), [size] * 4 + [2 * size])
    two1, came0, parts1 = bar((two1, came0, parts1))
    up_top, up_low, down_top, down_low, mine = parts1
    early = shift(up_low, 1), shift(down_top, -1)
    far1, far = forward(two1, [size] * 2)
    relays = shift(far[0], 1), shift(far[1], -1)
    came0, _ = bar((came0, far))
    total0 = merge(mine0.astype(F32) + came0[0].astype(F32), came0[1])
    send_home0 = by_device(total0, experts)
    home0 = swap(send_home0)
    came_top = shift(merge(up_top, relays[0]), 1)
    came_low = shift(merge(down_low, relays[1]), -1)
    came_up = jnp.concatenate([came_top, early[0]], axis=0).astype(F32)
    came_down = jnp.concatenate([early[1], came_low], axis=0)
    group0, _ = bar((group0, send_home0))
    sums = grads(group0, (0.0, 0.0, 0.0))
    total1, home0, sums = bar((merge(mine.astype(F32) + came_up, came_down), home0, sums))
    send_home1 = by_device(total1, experts)
    home1 = swap(send_home1)

    d_tokens, d_weight = 0.0, 0.0
    for (seats, combine), home in zip(tables, (home0, home1)):
        home = home.reshape(seats.shape[1], width + LANES)
        d_tokens = d_tokens + dot(combine, home[:, :width], 1, 0)
        extra = home[:, width:].astype(F32)
        d_seat = jnp.where(seats, (extra[:, 0] + extra[:, 1])[None, :], 0.0)
        d_weight = d_weight + jnp.sum(d_seat.reshape(tok_dev, experts, -1), axis=2)
    d_tokens = d_tokens.astype(BF16)
    d_gates = jnp.sum(jnp.where(named, d_weight[:, None, :], 0.0), axis=2)

    near1, far1, _ = bar((near1, far1, send_home1))
    grad_gate, grad_up, grad_down = grads(far1, grads(near1, sums))
    grad_gate, grad_up, grad_down = [
        value.astype(BF16)[None] for value in (grad_gate, grad_up, grad_down)
    ]
    return d_tokens, d_gates, grad_gate, grad_up, grad_down


def solution(mesh):
    rows = P(("dp", "node", "local"), None)
    wide = P(("node", "local"), None, "dp")
    tall = P(("node", "local"), "dp", None)
    return jax.shard_map(
        local,
        mesh=mesh,
        in_specs=(rows, rows, rows, rows, wide, wide, tall),
        out_specs=(rows, rows, wide, wide, tall),
        check_vma=False,
    )
```

```python
import jax
import jax.numpy as jnp
from jax import lax
from jax.experimental import pallas as pl
from jax.experimental.pallas import tpu as pltpu
from jax.sharding import PartitionSpec as P

F32 = jnp.float32
BF16 = jnp.bfloat16
GROUP_MAX = 4
LANES = 128
CHUNK = 1792


def shift(value, step):
    size = lax.axis_size("dp")
    return lax.ppermute(value, "dp", [(i, (i + step) % size) for i in range(size)])


def swap(value):
    return lax.all_to_all(value, ("node", "local"), split_axis=0, concat_axis=0, tiled=True)


def by_device(value, peers):
    return value.reshape(peers, -1, LANES)


def dot(a, b, ca, cb):
    return lax.dot_general(a, b, (((ca,), (cb,)), ((), ())), preferred_element_type=F32)


def expert_kernel(steps, count, *refs):
    x_refs, dy_refs, refs = refs[:count], refs[count:2 * count], refs[2 * count:]
    gate_ref, up_ref, down_ref, d_gate_ref, d_up_ref, hidden_ref = refs[:6]
    out_refs, (gate_acc, up_acc, d_hidden_acc) = refs[6:-3], refs[-3:]

    def put(value, begin):
        first = 0
        for ref in out_refs:
            last = first + ref.shape[0]
            ref[:, pl.ds(begin, value.shape[1])] = value[first:last]
            first = last
    phase, step = pl.program_id(0), pl.program_id(1)

    @pl.when(phase == 0)
    def _():
        @pl.when(step == 0)
        def _():
            gate_acc[...] = jnp.zeros_like(gate_acc)
            up_acc[...] = jnp.zeros_like(up_acc)
            d_hidden_acc[...] = jnp.zeros_like(d_hidden_acc)

        rows_x = jnp.concatenate([ref[...] for ref in x_refs], axis=0)
        rows_dy = jnp.concatenate([ref[...] for ref in dy_refs], axis=0)
        gate_acc[...] += dot(rows_x, gate_ref[...], 1, 0)
        up_acc[...] += dot(rows_x, up_ref[...], 1, 0)
        d_hidden_acc[...] += dot(rows_dy, down_ref[...], 1, 1)

        @pl.when(step == steps - 1)
        def _():
            gate_pre, up_pre, d_hidden = gate_acc[...], up_acc[...], d_hidden_acc[...]
            sigmoid_gate = jax.nn.sigmoid(gate_pre)
            activated = gate_pre * sigmoid_gate
            hidden = (activated * up_pre).astype(BF16)
            hidden_ref[...] = hidden
            d_gate_ref[...] = (
                d_hidden * up_pre * sigmoid_gate * (1.0 + gate_pre * (1.0 - sigmoid_gate))
            ).astype(BF16)
            d_up_ref[...] = (d_hidden * activated).astype(BF16)
            gate_rows = jnp.sum(hidden.astype(F32) * d_hidden, axis=1, keepdims=True)
            high = gate_rows.astype(BF16).astype(F32)
            lane = lax.broadcasted_iota(jnp.int32, (gate_rows.shape[0], LANES), 1)
            extra = jnp.where(lane == 0, high, jnp.where(lane == 1, gate_rows - high, 0.0))
            put(extra.astype(BF16), steps * CHUNK)

    @pl.when(phase == 1)
    def _():
        value = dot(d_gate_ref[...], gate_ref[...], 1, 1) + dot(d_up_ref[...], up_ref[...], 1, 1)
        put(value.astype(BF16), pl.multiple_of(step * CHUNK, CHUNK))


def expert_rows(blocks, sizes, gate_mat, up_mat, down_mat):
    width, hidden_width = gate_mat.shape
    steps = width // CHUNK
    rows = sum(block.shape[0] for block in blocks)
    small = jax.ShapeDtypeStruct((rows, hidden_width), BF16)
    whole = pl.BlockSpec((rows, hidden_width), lambda p, k: (0, 0))

    def part(block, first):
        return pl.BlockSpec(
            (block.shape[0], CHUNK), lambda p, k: (0, first + k * (1 - p) + (steps - 1) * p)
        )

    return pl.pallas_call(
        lambda *refs: expert_kernel(steps, len(blocks), *refs),
        grid=(2, steps),
        in_specs=[part(block, 0) for block in blocks]
        + [part(block, steps) for block in blocks]
        + [
            pl.BlockSpec((CHUNK, hidden_width), lambda p, k: (k, 0)),
            pl.BlockSpec((CHUNK, hidden_width), lambda p, k: (k, 0)),
            pl.BlockSpec((hidden_width, CHUNK), lambda p, k: (0, k * (1 - p) + (steps - 1) * p)),
        ],
        out_specs=[whole] * 3
        + [pl.BlockSpec((size, width + LANES), lambda p, k: (0, 0)) for size in sizes],
        out_shape=[small] * 3
        + [jax.ShapeDtypeStruct((size, width + LANES), BF16) for size in sizes],
        scratch_shapes=[pltpu.VMEM((rows, hidden_width), F32)] * 3,
        compiler_params=pltpu.CompilerParams(vmem_limit_bytes=60 * 1024 * 1024),
        cost_estimate=pl.CostEstimate(flops=1000000, bytes_accessed=1000000, transcendentals=0),
    )(*blocks, *blocks, gate_mat, up_mat, down_mat)


def local(tokens, cotangent, routes, gates, w_gate, w_up, w_down):
    tok_dev, width = tokens.shape
    top = routes.shape[1]
    nodes = lax.axis_size("node")
    experts = nodes * lax.axis_size("local")
    group_rows = tok_dev * min(GROUP_MAX, nodes) // nodes
    most = min(group_rows, max(2, tok_dev * top // experts + 1))

    named = routes[:, :, None] == jnp.arange(experts, dtype=jnp.int32)
    member = jnp.any(named, axis=1)
    member_i = member.astype(jnp.int32)
    rank = jnp.cumsum(member_i, axis=0) - member_i
    rank = jnp.where(member, rank, most).astype(BF16)
    weight = jnp.sum(jnp.where(named, gates.astype(F32)[:, :, None], 0.0), axis=1)

    def seat_table(first, count):
        columns = experts * count
        spread = lax.broadcasted_iota(jnp.int32, (experts, columns), 1) // count
        spread = (spread == lax.broadcasted_iota(jnp.int32, (experts, columns), 0)).astype(BF16)
        seat_of = lax.broadcasted_iota(jnp.int32, (tok_dev, columns), 1) % count + first
        seats = dot(rank, spread, 1, 0).astype(jnp.int32) == seat_of
        return seats, jnp.where(seats, dot(weight.astype(BF16), spread, 1, 0), 0.0).astype(BF16)

    tables = [seat_table(0, 1), seat_table(1, most - 1)]
    both = jnp.concatenate([tokens, cotangent], axis=1)

    down_mat = w_down[0]
    hidden_width = down_mat.shape[0]
    bar = lax.optimization_barrier

    def pick(turn):
        return by_device(dot(tables[turn][0].astype(BF16), both, 0, 0).astype(BF16), experts)

    def flat(raw, columns):
        return raw.reshape(-1, columns)

    def ring_one(own):
        return shift(own, -1), shift(own, 1)

    def ring_two(up, down):
        size = up.shape[0] // 2
        return shift(up[:size], -1), shift(down[size:], 1)

    def forward(blocks, sizes):
        d_gate_pre, d_up_pre, hidden, *parts = expert_rows(blocks, sizes, w_gate[0], w_up[0], down_mat)
        return (blocks, d_gate_pre, d_up_pre, hidden), parts

    def merge(first, second):
        return (first.astype(F32) + second.astype(F32)).astype(BF16)

    def grads(saved, sums):
        blocks, d_gate_pre, d_up_pre, hidden = saved
        rows_x = jnp.concatenate([block[:, :width] for block in blocks], axis=0)
        rows_dy = jnp.concatenate([block[:, width:] for block in blocks], axis=0)
        return (
            sums[0] + dot(rows_x, d_gate_pre, 0, 0),
            sums[1] + dot(rows_x, d_up_pre, 0, 0),
            sums[2] + dot(hidden, rows_dy, 0, 0),
        )

    raw0 = swap(pick(0))
    send1, raw0 = bar((pick(1), raw0))
    own0 = flat(raw0, 2 * width)
    one0 = ring_one(own0)
    raw1 = swap(send1)
    two0 = ring_two(*one0)
    own0, one0, two0, raw1 = bar((own0, one0, two0, raw1))
    own1 = flat(raw1, 2 * width)
    one1 = ring_one(own1)
    size = own0.shape[0] // 2
    group0, parts0 = forward(two0 + one0 + (own0,), [size] * 6 + [2 * size])
    far_top, far_low, up_top, up_low, down_top, down_low, mine0 = parts0
    relays0 = shift(far_top, 1), shift(far_low, -1)
    own1, one1, up_top, up_low, down_top, down_low, mine0 = bar(
        (own1, one1, up_top, up_low, down_top, down_low, mine0)
    )
    two1 = ring_two(*one1)
    up0 = jnp.concatenate([merge(up_top, relays0[0]), up_low], axis=0)
    down0 = jnp.concatenate([down_top, merge(down_low, relays0[1])], axis=0)
    up0, down0, own1, one1 = bar((up0, down0, own1, one1))
    came0 = shift(up0, 1), shift(down0, -1)
    size = own1.shape[0] // 2
    near1, parts1 = forward(one1 + (own1,), [size] * 4 + [2 * size])
    two1, parts1 = bar((two1, parts1))
    up_top, up_low, down_top, down_low, mine = parts1
    early = shift(up_low, 1), shift(down_top, -1)
    far1, far = forward(two1, [size] * 2)
    relays = shift(far[0], 1), shift(far[1], -1)
    came0, _ = bar((came0, far))
    total0 = merge(mine0.astype(F32) + came0[0].astype(F32), came0[1])
    send_home0 = by_device(total0, experts)
    home0 = swap(send_home0)
    came_top = shift(merge(up_top, relays[0]), 1)
    came_low = shift(merge(down_low, relays[1]), -1)
    came_up = jnp.concatenate([came_top, early[0]], axis=0).astype(F32)
    came_down = jnp.concatenate([early[1], came_low], axis=0)
    group0, _ = bar((group0, send_home0))
    sums = grads(group0, (0.0, 0.0, 0.0))
    total1, home0, sums = bar((merge(mine.astype(F32) + came_up, came_down), home0, sums))
    send_home1 = by_device(total1, experts)
    home1 = swap(send_home1)

    d_tokens, d_weight = 0.0, 0.0
    for (seats, combine), home in zip(tables, (home0, home1)):
        home = home.reshape(seats.shape[1], width + LANES)
        d_tokens = d_tokens + dot(combine, home[:, :width], 1, 0)
        extra = home[:, width:].astype(F32)
        d_seat = jnp.where(seats, (extra[:, 0] + extra[:, 1])[None, :], 0.0)
        d_weight = d_weight + jnp.sum(d_seat.reshape(tok_dev, experts, -1), axis=2)
    d_tokens = d_tokens.astype(BF16)
    d_gates = jnp.sum(jnp.where(named, d_weight[:, None, :], 0.0), axis=2)

    near1, far1, _ = bar((near1, far1, send_home1))
    grad_gate, grad_up, grad_down = grads(far1, grads(near1, sums))
    grad_gate, grad_up, grad_down = [
        value.astype(BF16)[None] for value in (grad_gate, grad_up, grad_down)
    ]
    return d_tokens, d_gates, grad_gate, grad_up, grad_down


def solution(mesh):
    rows = P(("dp", "node", "local"), None)
    wide = P(("node", "local"), None, "dp")
    tall = P(("node", "local"), "dp", None)
    return jax.shard_map(
        local,
        mesh=mesh,
        in_specs=(rows, rows, rows, rows, wide, wide, tall),
        out_specs=(rows, rows, wide, wide, tall),
        check_vma=False,
    )
```
